32 devices in a mesh: groups: 2 (over y), dp: 4 (over x, core), expert: 4 (over z).
Axes of the slice: x: 2, y: 2, z: 4, core: 2. Of those that a mesh axis runs over, the one named last changes fastest.
Arguments:
- tokens: bfloat16 [256, 2048], P(('groups', 'dp', 'expert')), parts along dimension 0, may hold values from -3.5 to 3.5
- routes: int32 [256, 8], P('groups'), parts along dimension 0, may hold values from 0 to 15, all different within a row; in each aligned block of 8 rows (0 to 7, 8 to 15, ...) at most 8 rows name the same one
- gates: float32 [256, 8], P(('groups', 'dp', 'expert')), parts along dimension 0, may hold values from 0.1 to 1
- valid: int32 [256], P('groups'), parts along dimension 0, may hold values 0 or 1
- norm_gain: float32 [2048], replicated, may hold values from 0.5 to 1.5
- final_gain: float32 [2048], replicated, may hold values from 0.5 to 1.5
- w_gate: bfloat16 [16, 2048, 1024], P('expert', None, 'dp'), may hold values from -0.125 to 0.125
- w_up: bfloat16 [16, 2048, 1024], P('expert', None, 'dp'), may hold values from -0.125 to 0.125
- w_down: bfloat16 [16, 1024, 2048], P('expert', 'dp'), may hold values from -0.1875 to 0.1875
- head_weight: bfloat16 [2048, 10240], P(None, ('dp', 'expert')), as said below
- student_logits: bfloat16 [256, 10240], P('groups', ('dp', 'expert')), parts along dimension 0, may hold values from -24 to 220
Outputs:
- reverse_kl: float32 [256], P('groups'), parts along dimension 0
- logit_grad: bfloat16 [256, 10240], P('groups', ('dp', 'expert')), parts along dimension 0
The draws below stay inside these ranges and needn't reach their ends.
There are 2 independent parts, one for each index of `groups`. The reference program is written for one: setup_inputs(seed, part) draws one part's arguments, and reference() takes and returns one part's arrays. A program takes and returns all parts, laid end to end along the dimension named above; an argument that names none is the same for every part. Nothing has to cross between parts.
Inputs may be any that keep to these rules, and one draw needn't show every extreme that they name: Each token names 8 different experts. In the 8 tokens of one device (aligned blocks of rows), no expert is named by more than 8 routes, a bound that some block reaches. `head_weight`: entries are of order one over the square root of 2048.
All inputs are finite; a program needn't handle non-finite values.
Results may differ from the reference program's by a relative error of at most 0.015.
Values may be sent and summed in bfloat16 or wider, within the bound.
A program may use at most 64 MiB of HBM per device.

```python
import math
import jax
import jax.numpy as jnp
import numpy as np
from jax import lax

D = 2048
FF = 1024
TOP = 8
TOK_DEV = 8
EXPERTS = 16
TOKENS = 128
VOCAB = 10240
CAP = 8
N_DP = 4
N_EXPERT = 4


def draw_tokens(key, part):
    noise_key = jax.random.fold_in(key, 0)
    noise_part = 0.5 * jax.random.normal(noise_key, (TOKENS, D), jnp.float32)
    return jnp.clip(noise_part, -3.0, 3.0).astype(jnp.bfloat16)


def draw_head_weight(key, part):
    noise_key = jax.random.fold_in(key, 0)
    rising = 1.0 + 2.0 * jnp.arange(VOCAB, dtype=jnp.float32) / VOCAB
    scale_root = jnp.sqrt(jnp.float32(D))
    noise_part = jnp.clip(jax.random.normal(noise_key, (D, VOCAB), jnp.float32), -4.0, 4.0)
    return (noise_part * rising[None, :] / scale_root).astype(jnp.bfloat16)


def draw_student_logits(key, part):
    subkeys = jax.random.split(key, 2)
    rising = 1.0 + 2.0 * jnp.arange(VOCAB, dtype=jnp.float32) / VOCAB
    row_scales = jnp.exp(jax.random.uniform(subkeys[0], (TOKENS, 1), jnp.float32, 0.0, jnp.log(2.0)))
    base_logits = 1.2 * jax.random.normal(subkeys[1], (TOKENS, VOCAB), jnp.float32) * rising[None, :] * row_scales
    return jnp.clip(base_logits, -14.0, 14.0).astype(jnp.bfloat16)


def plant(result, rng, least, largest):
    longest = result.shape.index(max(result.shape))
    spots = []
    for shift in (0, 1):
        where = [jax.random.randint(jax.random.fold_in(rng, axis), (), 0, length) for axis, length in enumerate(result.shape)]
        where[longest] = (where[longest] + shift) % result.shape[longest]
        spots.append(tuple(where))
    return result.at[spots[0]].set(least).at[spots[1]].set(largest)


def shard_levels(own_key, shape, pieces, smallest, largest):
    level, own = 1.0, jax.random.fold_in(own_key, 6)
    for axis_at, parts in pieces:
        heights = jnp.exp(jax.random.uniform(jax.random.fold_in(own, axis_at), (parts,), jnp.float32, smallest / len(pieces), largest / len(pieces)))
        level = level * jnp.repeat(heights, shape[axis_at] // parts).reshape([-1 if axis == axis_at else 1 for axis in range(len(shape))])
    return level


def assign_block(stream_key, own, number, rows, amount, top, limit, lean):
    order = jax.random.permutation(stream_key, amount)
    heavy_load, ordinary = portions_of(amount, rows * top, limit, lean, True), portions_of(amount, rows * top, limit, lean, False)
    places = jnp.arange(amount)

    def named(lengths, rotation):
        used = int((lengths > 0).sum())
        fixed = max(1, used // 4)
        shifted = fixed + (places - fixed + rotation * (used - fixed)) % max(1, amount - fixed)
        return jnp.zeros((amount,), jnp.int32).at[order[jnp.where(places < fixed, places, shifted)]].set(jnp.asarray(lengths, jnp.int32))

    lengths = jnp.where(number % 4 == 0, named(heavy_load, number // 4), named(ordinary, number - number // 4 - 1))
    mixed = jax.random.permutation(jax.random.fold_in(own, 3), amount)
    source_of, taker = mixed[0:amount // 2 * 2:2], mixed[1:amount // 2 * 2:2]
    room = jnp.minimum(lengths[source_of] - 1, limit - lengths[taker]) // 2
    room = jnp.where((source_of == order[0]) | (taker == order[0]) | (lengths[taker] == 0), 0, jnp.maximum(room, 0))
    shifted = jax.random.randint(jax.random.fold_in(own, 4), (amount // 2,), 0, 1 << 20) % (room + 1)
    lengths = lengths.at[source_of].add(-shifted).at[taker].add(shifted)
    members = jnp.searchsorted(jnp.cumsum(lengths), jnp.arange(rows * top), side="right").astype(jnp.int32)
    table = members.reshape(top, rows).T
    table = table[jax.random.permutation(jax.random.fold_in(own, 1), rows)]
    rotation = jax.random.randint(jax.random.fold_in(own, 2), (rows, 1), 0, top)
    return jnp.take_along_axis(table, (jnp.arange(top)[None, :] + rotation) % top, axis=1)


def portions_of(count, total, reach, lean, full):
    loads = [(1 << 20) // math.isqrt(grade ** lean) + 1 for grade in range(1, count + 1)]
    largest = reach if full else min(reach, max(-(-total // count), total * loads[0] // sum(loads)))
    least = 1 if total - largest >= count - 1 else 0
    holding, spare = [largest] + [least] * (count - 1), total - largest - least * (count - 1)
    while spare > 0:
        free = [i for i in range(1, count) if holding[i] < largest] or [i for i in range(1, count) if holding[i] < reach]
        pool, budget = sum([loads[i] for i in free]), spare
        for i in free:
            extra = min(reach - holding[i], max(1, budget * loads[i] // pool), spare)
            holding[i] = holding[i] + extra
            spare = spare - extra
    return np.array(holding)


def normal_values(stream_key, shape, scale, most, pieces=(), held_as=jnp.bfloat16):
    entries = jax.random.normal(stream_key, shape, jnp.float32) * scale
    if len(pieces) > 0:
        entries = shard_levels(stream_key, shape, pieces, -0.22, 0.18) * entries
    return jnp.clip(entries, min=-most, max=most).astype(held_as)


def setup_inputs(seed: int = 0, part: int = 0) -> dict:
    splits = jax.random.split(jax.random.key(seed), 12)
    part_splits = jax.random.split(jax.random.fold_in(splits[11], part), 12)
    tokens = draw_tokens(jax.random.fold_in(jax.random.fold_in(splits[11], part), 71), part)
    routes_keys = jax.random.split(jax.random.fold_in(part_splits[1], 1), TOKENS // TOK_DEV)
    routes_turns = jax.random.permutation(jax.random.fold_in(part_splits[1], 3), TOKENS // TOK_DEV)
    routes = jax.vmap(lambda own, number: assign_block(jax.random.fold_in(part_splits[1], 2), own, number, TOK_DEV, EXPERTS, TOP, CAP, 2))(routes_keys, routes_turns).reshape((TOKENS, TOP))
    gates = jnp.clip(jnp.exp(math.log(1.0) - 2.3025851 * jax.random.uniform(part_splits[2], (TOKENS, TOP), jnp.float32) ** shard_levels(part_splits[2], (TOKENS, TOP), ((0, 16),), -0.2, 0.2)), 0.1, 1.0)
    valid = plant((jax.random.randint(part_splits[3], (TOKENS,), 0, 4) < 3).astype(jnp.int32), jax.random.fold_in(part_splits[3], 1), 0, 1)
    norm_gain = jnp.clip(1.0 + 0.1 * jax.random.normal(splits[4], (D,), jnp.float32), 0.5, 1.5)
    final_gain = jnp.clip(1.0 + 0.1 * jax.random.normal(splits[5], (D,), jnp.float32), 0.5, 1.5)
    w_gate = normal_values(splits[6], (EXPERTS, D, FF), D ** -0.5, 0.125, ((0, 4), (2, 4)))
    w_up = normal_values(splits[7], (EXPERTS, D, FF), D ** -0.5, 0.125, ((0, 4), (2, 4)))
    w_down = normal_values(splits[8], (EXPERTS, FF, D), FF ** -0.5, 0.1875, ((0, 4), (1, 4)))
    head_weight = draw_head_weight(jax.random.fold_in(splits[11], 71), part)
    student_logits = draw_student_logits(jax.random.fold_in(jax.random.fold_in(splits[11], part), 71), part)
    return {"tokens": tokens, "routes": routes, "gates": gates, "valid": valid, "norm_gain": norm_gain, "final_gain": final_gain, "w_gate": w_gate, "w_up": w_up, "w_down": w_down, "head_weight": head_weight, "student_logits": student_logits}


epsilon = 1e-06

def rms_scale(values, gain_vector):
    mean_square = lax.optimization_barrier(jnp.mean(values * values, axis=-1, keepdims=True))
    return values * lax.rsqrt(mean_square + epsilon) * gain_vector

def reference(tokens, routes, gates, valid, norm_gain, final_gain, w_gate, w_up, w_down, head_weight, student_logits):
    hidden_in = tokens.astype(jnp.float32)
    normed = rms_scale(hidden_in, norm_gain).astype(jnp.bfloat16)
    weights = gates / lax.optimization_barrier(jnp.sum(gates, axis=1, keepdims=True))
    flat_routes = routes.reshape(-1)
    flat_weights = weights.reshape(-1)
    route_total = TOKENS * TOP
    most_rows = CAP * N_DP * N_EXPERT

    def one_expert(combined, expert):
        picked = jnp.nonzero(flat_routes == expert, size=most_rows, fill_value=route_total)[0].astype(jnp.int32)
        live_rows = picked < route_total
        token_ids = jnp.minimum(picked // TOP, TOKENS - 1).astype(jnp.int32)
        row_block = normed[token_ids]
        gate_part = jnp.dot(row_block, w_gate[expert], preferred_element_type=jnp.float32)
        up_part = jnp.dot(row_block, w_up[expert], preferred_element_type=jnp.float32)
        activation = (jax.nn.silu(gate_part) * up_part).astype(jnp.bfloat16)
        expert_out = jnp.dot(activation, w_down[expert], preferred_element_type=jnp.float32).astype(jnp.bfloat16)
        expert_out = lax.optimization_barrier(expert_out).astype(jnp.float32)
        safe_index = jnp.minimum(picked, route_total - 1).astype(jnp.int32)
        route_scale = jnp.where(live_rows, flat_weights[safe_index], jnp.zeros_like(flat_weights[safe_index]))
        combined = combined.at[token_ids].add(route_scale[:, None] * expert_out)
        return (combined, None)
    combined, _ = lax.scan(one_expert, jnp.zeros((TOKENS, D), jnp.float32), jnp.arange(EXPERTS, dtype=jnp.int32))
    mixed = hidden_in + combined
    final_normed = rms_scale(mixed, final_gain).astype(jnp.bfloat16)
    teacher = jnp.dot(final_normed, head_weight, preferred_element_type=jnp.float32)
    student = student_logits.astype(jnp.float32)
    teacher_top = lax.optimization_barrier(jnp.max(teacher, axis=1, keepdims=True))
    student_top = lax.optimization_barrier(jnp.max(student, axis=1, keepdims=True))
    log_teacher = teacher_top + jnp.log(lax.optimization_barrier(jnp.sum(jnp.exp(teacher - teacher_top), axis=1, keepdims=True)))
    log_student = student_top + jnp.log(lax.optimization_barrier(jnp.sum(jnp.exp(student - student_top), axis=1, keepdims=True)))
    student_prob = jnp.exp(student - log_student)
    divergence = lax.optimization_barrier(jnp.sum(student_prob * (student - teacher), axis=1, keepdims=True)) - log_student + log_teacher
    valid_rows = valid.astype(jnp.float32)[:, None]
    logit_grad = (valid_rows * student_prob * (student - log_student - (teacher - log_teacher) - divergence)).astype(jnp.bfloat16)
    return ((valid_rows * divergence)[:, 0], logit_grad)
```

```python
import functools

import jax
import jax.numpy as jnp
from jax import lax
from jax.experimental import pallas as pl
from jax.experimental.pallas import tpu as pltpu
from jax.sharding import PartitionSpec as P

epsilon = 1e-06
F32, BF16 = jnp.float32, jnp.bfloat16
LANES = 128


def kernel(
    n_dp,
    n_ex,
    tok_ref,
    routes_ref,
    gates_ref,
    valid_ref,
    ng_ref,
    fg_ref,
    wg_hbm,
    wu_hbm,
    wd_hbm,
    hw_hbm,
    st_hbm,
    kl_ref,
    grad_ref,
    wg,
    wu,
    wd,
    hw,
    st,
    xbuf,
    act,
    yb,
    cbuf,
    sbuf,
    rbuf,
    zbuf,
    stat,
    teach,
    load_sem,
    x_send,
    x_recv,
    x_fwd,
    c_send,
    c_recv,
    r_send,
    r_recv,
    z_send,
    z_recv,
    z_fwd,
    s_send,
    s_recv,
):
    grp, dp, ex = lax.axis_index("groups"), lax.axis_index("dp"), lax.axis_index("expert")
    core = lax.rem(dp, 2)
    col = lax.div(dp, 2)
    n_dev = n_dp * n_ex
    n_chip = n_dev // 2
    me = dp * n_ex + ex
    chip = col * n_ex + ex
    per, width = tok_ref.shape
    half = width // 2
    total = n_dev * per
    rows = min(total, 128)
    blocks = rows // per
    local = wg.shape[0]
    hidden = wg.shape[2]

    def device(position):
        return (grp, lax.div(position, n_ex), lax.rem(position, n_ex))

    def at_chip(q, c):
        return (2 * lax.div(q, n_ex) + c) * n_ex + lax.rem(q, n_ex)

    sibling = at_chip(chip, 1 - core)

    def remote(src, dst, send, recv, position):
        return pltpu.make_async_remote_copy(
            src_ref=src,
            dst_ref=dst,
            send_sem=send,
            recv_sem=recv,
            device_id=device(position),
            device_id_type=pl.DeviceIdType.MESH,
        )

    loads = [
        pltpu.make_async_copy(src, dst, load_sem.at[i])
        for i, (src, dst) in enumerate(
            ((wg_hbm, wg), (wu_hbm, wu), (wd_hbm, wd), (st_hbm, st), (hw_hbm, hw))
        )
    ]
    for load in loads:
        load.start()

    barrier = pltpu.get_barrier_semaphore()

    def greet(k, carry):
        pl.semaphore_signal(
            barrier,
            inc=1,
            device_id=device(lax.rem(me + k, n_dev)),
            device_id_type=pl.DeviceIdType.MESH,
        )
        return carry

    lax.fori_loop(1, n_dev, greet, 0)

    x = tok_ref[...].astype(F32)
    normed = x * lax.rsqrt(jnp.mean(x * x, axis=-1, keepdims=True) + epsilon) * ng_ref[...]
    gates = gates_ref[...]
    weights = gates / jnp.sum(gates, axis=1, keepdims=True)
    own_routes = routes_ref[pl.ds(pl.multiple_of(me * per, per), per), :]
    lane = lax.broadcasted_iota(jnp.int32, (per, LANES), 1)
    dense = jnp.zeros((per, LANES), F32)
    for k in range(gates.shape[1]):
        dense += jnp.where(lane == own_routes[:, k : k + 1], weights[:, k : k + 1], 0.0)
    high = dense.astype(BF16).astype(F32)
    xbuf[me, :, 0:half] = jnp.concatenate([normed[:, :half], normed[:, half:]], axis=0).astype(BF16)
    xbuf[me, :, half : half + LANES] = jnp.concatenate([high, dense - high], axis=0).astype(BF16)

    pl.semaphore_wait(barrier, n_dev - 1)

    def gather(buf, send, recv, fwd):
        def direct(k):
            position = at_chip(lax.rem(chip + k, n_chip), core)
            return remote(buf.at[me], buf.at[me], send.at[k], recv.at[me], position)

        to_sibling = remote(buf.at[me], buf.at[me], send.at[0], recv.at[me], sibling)

        def arrival(position):
            return remote(buf.at[position], buf.at[position], send.at[0], recv.at[position], sibling)

        def forward(k):
            position = at_chip(lax.rem(chip + n_chip - k, n_chip), core)
            return remote(buf.at[position], buf.at[position], fwd.at[k], recv.at[position], sibling)

        def start(k, carry):
            direct(k).start()
            return carry

        def relay(k, carry):
            arrival(at_chip(lax.rem(chip + n_chip - k, n_chip), core)).wait_recv()
            forward(k).start()
            return carry

        def collect(k, carry):
            arrival(at_chip(lax.rem(chip + n_chip - k, n_chip), 1 - core)).wait_recv()
            return carry

        def finish(k, carry):
            direct(k).wait_send()
            forward(k).wait_send()
            return carry

        lax.fori_loop(1, n_chip, start, 0)
        to_sibling.start()
        lax.fori_loop(1, n_chip, relay, 0)
        lax.fori_loop(0, n_chip, collect, 0)

        def done():
            to_sibling.wait_send()
            lax.fori_loop(1, n_chip, finish, 0)

        return done

    finish_x = gather(xbuf, x_send, x_recv, x_fwd)

    loads[0].wait()
    loads[1].wait()
    loads[2].wait()

    def experts(r, carry):
        first = pl.multiple_of(r * blocks, blocks)
        packed = xbuf[pl.ds(first, blocks)].astype(F32)
        low = packed[:, 0:per, :].reshape(rows, half + LANES)
        top = packed[:, per : 2 * per, :].reshape(rows, half + LANES)
        inputs = jnp.concatenate([low[:, :half], top[:, :half]], axis=1).astype(BF16)
        scales = low[:, half:] + top[:, half:]
        where = lax.broadcasted_iota(jnp.int32, (rows, LANES), 1)
        for j in range(local):
            scale = jnp.sum(
                jnp.where(where == ex * local + j, scales, 0.0), axis=1, keepdims=True
            )
            gate = jnp.dot(inputs, wg[j], preferred_element_type=F32)
            up = jnp.dot(inputs, wu[j], preferred_element_type=F32)
            out = gate / (1.0 + jnp.exp(-gate)) * up * scale
            act[:, j * hidden : (j + 1) * hidden] = out.astype(BF16)
        step = min(half, 512)
        for n in range(half // step):
            pair = []
            for base in (0, half):
                part = None
                lo = base + n * step
                down = wd[:, :, lo : lo + step].reshape(local * hidden, step)
                part = jnp.dot(act[...], down, preferred_element_type=F32)
                pair.append(part.reshape(blocks, per, step))
            yb[pl.ds(first, blocks), :, n * step : (n + 1) * step] = jnp.concatenate(
                pair, axis=1
            ).astype(BF16)
        return carry

    lax.fori_loop(0, total // rows, experts, 0)

    def half_sum(c):
        src = pl.multiple_of((2 * c + 1 - core) * n_ex, n_ex)
        return remote(
            yb.at[pl.ds(src, n_ex)],
            cbuf.at[pl.ds(pl.multiple_of(c * n_ex, n_ex), n_ex)],
            c_send.at[c],
            c_recv.at[c],
            sibling,
        )

    for c in range(n_dp // 2):
        half_sum(c).start()
    for c in range(n_dp // 2):
        half_sum(c).wait_recv()

    def scatter(k):
        q = lax.rem(chip + k, n_chip)
        return remote(
            sbuf.at[q], rbuf.at[chip], r_send.at[k], r_recv.at[chip], at_chip(q, core)
        )

    def scatter_from(q):
        return remote(sbuf.at[q], rbuf.at[q], r_send.at[0], r_recv.at[q], at_chip(q, core))

    def add_and_send(k, carry):
        q = lax.rem(chip + k, n_chip)
        sbuf[q] = (yb[at_chip(q, core)].astype(F32) + cbuf[q].astype(F32)).astype(BF16)
        scatter(k).start()
        return carry

    lax.fori_loop(1, n_chip, add_and_send, 0)
    mine = yb[me].astype(F32) + cbuf[chip].astype(F32)

    def take(k, acc):
        q = lax.rem(chip + n_chip - k, n_chip)
        scatter_from(q).wait_recv()
        return acc + rbuf[q].astype(F32)

    mine = lax.fori_loop(1, n_chip, take, mine)
    mixed_low = x[:, :half] + mine[:per]
    mixed_top = x[:, half:] + mine[per:]
    square = jnp.sum(mixed_low * mixed_low + mixed_top * mixed_top, axis=-1, keepdims=True)
    inverse = lax.rsqrt(square / width + epsilon)
    zbuf[me] = jnp.concatenate(
        [mixed_low * inverse * fg_ref[:, :half], mixed_top * inverse * fg_ref[:, half:]], axis=0
    ).astype(BF16)

    finish_z = gather(zbuf, z_send, z_recv, z_fwd)
    loads[3].wait()
    loads[4].wait()

    def head(r, carry):
        first = pl.multiple_of(r * blocks, blocks)
        span = pl.ds(pl.multiple_of(r * rows, rows), rows)
        packed = zbuf[pl.ds(first, blocks)].astype(F32)
        low = packed[:, 0:per, :].reshape(rows, half)
        top = packed[:, per : 2 * per, :].reshape(rows, half)
        inputs = jnp.concatenate([low, top], axis=1).astype(BF16)
        teacher = jnp.dot(inputs, hw[...], preferred_element_type=F32)
        teach[span, :] = teacher
        student = st[span, :].astype(F32)
        t_top = jnp.max(teacher, axis=1, keepdims=True)
        s_top = jnp.max(student, axis=1, keepdims=True)
        t_sum = jnp.sum(jnp.exp(teacher - t_top), axis=1, keepdims=True)
        s_exp = jnp.exp(student - s_top)
        s_sum = jnp.sum(s_exp, axis=1, keepdims=True)
        cross = jnp.sum(s_exp * (student - teacher), axis=1, keepdims=True)
        where = lax.broadcasted_iota(jnp.int32, (rows, LANES), 1)
        table = jnp.zeros((rows, LANES), F32)
        for i, value in enumerate((t_top, t_sum, s_top, s_sum, cross)):
            table = jnp.where(where == i, value, table)
        stat[me, :, span] = table.T[0:8]
        return carry

    lax.fori_loop(0, total // rows, head, 0)

    def tell(k):
        position = lax.rem(me + k, n_dev)
        return remote(stat.at[me], stat.at[me], s_send.at[k], s_recv.at[me], position)

    def heard(k):
        position = lax.rem(me + k, n_dev)
        return remote(stat.at[position], stat.at[position], s_send.at[0], s_recv.at[position], sibling)

    def tell_all(k, carry):
        tell(k).start()
        return carry

    def hear_all(k, carry):
        heard(k).wait_recv()
        return carry

    lax.fori_loop(1, n_dev, tell_all, 0)
    lax.fori_loop(1, n_dev, hear_all, 0)

    def final(r, carry):
        span = pl.ds(pl.multiple_of(r * rows, rows), rows)
        t_tops, t_sums = stat[:, 0, span], stat[:, 1, span]
        s_tops, s_sums, crosses = stat[:, 2, span], stat[:, 3, span], stat[:, 4, span]
        t_top = jnp.max(t_tops, axis=0, keepdims=True)
        s_top = jnp.max(s_tops, axis=0, keepdims=True)
        t_total = jnp.sum(jnp.exp(t_tops - t_top) * t_sums, axis=0, keepdims=True)
        s_scale = jnp.exp(s_tops - s_top)
        s_total = jnp.sum(s_scale * s_sums, axis=0, keepdims=True)
        cross = jnp.sum(s_scale * crosses, axis=0, keepdims=True)
        log_t = t_top + jnp.log(t_total)
        log_s = s_top + jnp.log(s_total)
        divergence = cross / s_total - log_s + log_t
        valid = valid_ref[:, span].astype(F32)
        kl_ref[:, span] = valid * divergence
        where = lax.broadcasted_iota(jnp.int32, (LANES, rows), 0)
        table = jnp.zeros((LANES, rows), F32)
        for i, value in enumerate((log_s, divergence - log_t + log_s, valid)):
            table = jnp.where(where == i, value, table)
        columns = table.T
        student = st[span, :].astype(F32)
        prob = columns[:, 2:3] * jnp.exp(student - columns[:, 0:1])
        grad_ref[span, :] = (prob * (student - teach[span, :] - columns[:, 1:2])).astype(BF16)
        return carry

    lax.fori_loop(0, total // rows, final, 0)

    finish_x()
    finish_z()
    for c in range(n_dp // 2):
        half_sum(c).wait_send()

    def finish_scatter(k, carry):
        scatter(k).wait_send()
        return carry

    def finish_tell(k, carry):
        tell(k).wait_send()
        return carry

    lax.fori_loop(1, n_chip, finish_scatter, 0)
    lax.fori_loop(1, n_dev, finish_tell, 0)


def body(
    n_dp,
    n_ex,
    tokens,
    routes,
    gates,
    valid,
    norm_gain,
    final_gain,
    w_gate,
    w_up,
    w_down,
    head_weight,
    student_logits,
):
    per, width = tokens.shape
    half = width // 2
    n_dev = n_dp * n_ex
    n_chip = n_dev // 2
    total, vocab = student_logits.shape
    local, _, hidden = w_gate.shape
    rows = min(total, 128)
    vmem = pl.BlockSpec(memory_space=pltpu.VMEM)
    hbm = pl.BlockSpec(memory_space=pl.ANY)
    dma = pltpu.SemaphoreType.DMA
    kl, grad = pl.pallas_call(
        functools.partial(kernel, n_dp, n_ex),
        out_shape=(
            jax.ShapeDtypeStruct((1, total), F32),
            jax.ShapeDtypeStruct((total, vocab), BF16),
        ),
        in_specs=[vmem] * 6 + [hbm] * 5,
        out_specs=(vmem, vmem),
        scratch_shapes=[
            pltpu.VMEM(w_gate.shape, BF16),
            pltpu.VMEM(w_up.shape, BF16),
            pltpu.VMEM(w_down.shape, BF16),
            pltpu.VMEM(head_weight.shape, BF16),
            pltpu.VMEM(student_logits.shape, BF16),
            pltpu.VMEM((n_dev, 2 * per, half + LANES), BF16),
            pltpu.VMEM((rows, local * hidden), BF16),
            pltpu.VMEM((n_dev, 2 * per, half), BF16),
            pltpu.VMEM((n_chip, 2 * per, half), BF16),
            pltpu.VMEM((n_chip, 2 * per, half), BF16),
            pltpu.VMEM((n_chip, 2 * per, half), BF16),
            pltpu.VMEM((n_dev, 2 * per, half), BF16),
            pltpu.VMEM((n_dev, 8, total), F32),
            pltpu.VMEM((total, vocab), F32),
            dma((5,)),
            dma((n_chip,)),
            dma((n_dev,)),
            dma((n_chip,)),
            dma((n_dp // 2,)),
            dma((n_dp // 2,)),
            dma((n_chip,)),
            dma((n_chip,)),
            dma((n_chip,)),
            dma((n_dev,)),
            dma((n_chip,)),
            dma((n_dev,)),
            dma((n_dev,)),
        ],
        compiler_params=pltpu.CompilerParams(
            collective_id=0, has_side_effects=True, vmem_limit_bytes=60 * 2**20
        ),
    )(
        tokens,
        routes,
        gates,
        valid.reshape(1, total),
        norm_gain.reshape(1, width),
        final_gain.reshape(1, width),
        w_gate,
        w_up,
        w_down,
        head_weight,
        student_logits,
    )
    return kl.reshape(total), grad


def solution(mesh):
    placed = (
        P(("groups", "dp", "expert"), None),
        P("groups", None),
        P(("groups", "dp", "expert"), None),
        P("groups"),
        P(),
        P(),
        P("expert", None, "dp"),
        P("expert", None, "dp"),
        P("expert", "dp", None),
        P(None, ("dp", "expert")),
        P("groups", ("dp", "expert")),
    )
    return jax.shard_map(
        functools.partial(body, mesh.shape["dp"], mesh.shape["expert"]),
        mesh=mesh,
        in_specs=placed,
        out_specs=(P("groups"), P("groups", ("dp", "expert"))),
        check_vma=False,
    )
```

```python
import functools

import jax
import jax.numpy as jnp
from jax import lax
from jax.experimental import pallas as pl
from jax.experimental.pallas import tpu as pltpu
from jax.sharding import PartitionSpec as P

epsilon = 1e-06
F32, BF16 = jnp.float32, jnp.bfloat16
LANES = 128


def kernel(
    n_dp,
    n_ex,
    tok_ref,
    routes_ref,
    gates_ref,
    valid_ref,
    ng_ref,
    fg_ref,
    wg_hbm,
    wu_hbm,
    wd_hbm,
    hw_hbm,
    st_hbm,
    kl_ref,
    grad_ref,
    wg,
    wu,
    wd,
    hw,
    st,
    xbuf,
    act,
    yb,
    cbuf,
    sxbuf,
    rxbuf,
    szbuf,
    rzbuf,
    zbuf,
    stat,
    teach,
    load_sem,
    x_z,
    x_x,
    x_c,
    x_recv,
    c_send,
    c_recv,
    rx_send,
    rx_recv,
    rz_send,
    rz_recv,
    z_z,
    z_x,
    z_c,
    z_recv,
    s_send,
    s_recv,
):
    grp, dp, ex = lax.axis_index("groups"), lax.axis_index("dp"), lax.axis_index("expert")
    core = lax.rem(dp, 2)
    col = lax.div(dp, 2)
    n_dev = n_dp * n_ex
    n_col = n_dp // 2
    me = dp * n_ex + ex
    per, width = tok_ref.shape
    half = width // 2
    total = n_dev * per
    rows = min(total, 128)
    blocks = rows // per
    local = wg.shape[0]
    hidden = wg.shape[2]

    def device(position):
        return (grp, lax.div(position, n_ex), lax.rem(position, n_ex))

    def at(x_col, c, z):
        return (2 * x_col + c) * n_ex + z

    def col_at(k):
        return lax.rem(col + k, n_col)

    def z_at(k):
        out, bit = ex, 1
        while bit < n_ex:
            if k & bit:
                out = out + bit - 2 * bit * lax.rem(lax.div(ex, bit), 2)
            bit *= 2
        return out

    sibling = at(col, 1 - core, ex)

    def remote(src, dst, send, recv, position):
        return pltpu.make_async_remote_copy(
            src_ref=src,
            dst_ref=dst,
            send_sem=send,
            recv_sem=recv,
            device_id=device(position),
            device_id_type=pl.DeviceIdType.MESH,
        )

    loads = [
        pltpu.make_async_copy(src, dst, load_sem.at[i])
        for i, (src, dst) in enumerate(
            ((wg_hbm, wg), (wu_hbm, wu), (wd_hbm, wd), (st_hbm, st), (hw_hbm, hw))
        )
    ]
    for load in loads:
        load.start()

    barrier = pltpu.get_barrier_semaphore()

    def greet(k, carry):
        pl.semaphore_signal(
            barrier,
            inc=1,
            device_id=device(lax.rem(me + k, n_dev)),
            device_id_type=pl.DeviceIdType.MESH,
        )
        return carry

    lax.fori_loop(1, n_dev, greet, 0)

    x = tok_ref[...].astype(F32)
    normed = x * lax.rsqrt(jnp.mean(x * x, axis=-1, keepdims=True) + epsilon) * ng_ref[...]
    gates = gates_ref[...]
    weights = gates / jnp.sum(gates, axis=1, keepdims=True)
    lane = lax.broadcasted_iota(jnp.int32, (per, LANES), 1)
    spot = lax.broadcasted_iota(jnp.int32, (per, total), 1)
    own = spot == lax.broadcasted_iota(jnp.int32, (per, total), 0) + me * per
    dense = jnp.zeros((per, LANES), F32)
    for k in range(gates.shape[1]):
        route = jnp.sum(
            jnp.where(own, routes_ref[k : k + 1, :], 0).astype(F32), axis=1, keepdims=True
        )
        dense += jnp.where(lane.astype(F32) == route, weights[:, k : k + 1], 0.0)
    high = dense.astype(BF16).astype(F32)
    xbuf[me, :, 0:half] = jnp.concatenate([normed[:, :half], normed[:, half:]], axis=0).astype(BF16)
    xbuf[me, :, half : half + LANES] = jnp.concatenate([high, dense - high], axis=0).astype(BF16)

    pl.semaphore_wait(barrier, n_dev - 1)

    def gather(buf, send_z, send_x, send_c, recv):
        def move(position, sem, target):
            return remote(buf.at[position], buf.at[position], sem, recv.at[position], target)

        started = []

        def start(position, sem, target):
            copy = move(position, sem, target)
            copy.start()
            started.append(copy)

        def arrive(position):
            move(position, send_c.at[0], sibling).wait_recv()

        def to_columns(position, kz):
            for kx in range(1, n_col):
                start(position, send_x.at[kz * n_col + kx], at(col_at(kx), core, ex))

        to_columns(me, 0)
        for kz in range(n_ex - 1, 0, -1):
            start(me, send_z.at[kz], at(col, core, z_at(kz)))
        start(me, send_c.at[0], sibling)
        for kz in range(1, n_ex):
            position = at(col, core, z_at(kz))
            arrive(position)
            to_columns(position, kz)
            start(position, send_c.at[kz * n_col], sibling)
        for kz in range(n_ex):
            for kx in range(1, n_col):
                position = at(col_at(n_col - kx), core, z_at(kz))
                arrive(position)
                start(position, send_c.at[kz * n_col + kx], sibling)
        for kz in range(n_ex):
            for kx in range(n_col):
                arrive(at(col_at(n_col - kx), 1 - core, z_at(kz)))
        return started

    sent = gather(xbuf, x_z, x_x, x_c, x_recv)

    loads[0].wait()
    loads[1].wait()
    loads[2].wait()

    def experts(r, carry):
        first = pl.multiple_of(r * blocks, blocks)
        packed = xbuf[pl.ds(first, blocks)].astype(F32)
        low = packed[:, 0:per, :].reshape(rows, half + LANES)
        top = packed[:, per : 2 * per, :].reshape(rows, half + LANES)
        inputs = jnp.concatenate([low[:, :half], top[:, :half]], axis=1).astype(BF16)
        scales = low[:, half:] + top[:, half:]
        where = lax.broadcasted_iota(jnp.int32, (rows, LANES), 1)
        for j in range(local):
            scale = jnp.sum(
                jnp.where(where == ex * local + j, scales, 0.0), axis=1, keepdims=True
            )
            gate = jnp.dot(inputs, wg[j], preferred_element_type=F32)
            up = jnp.dot(inputs, wu[j], preferred_element_type=F32)
            out = gate / (1.0 + jnp.exp(-gate)) * up * scale
            act[:, j * hidden : (j + 1) * hidden] = out.astype(BF16)
        step = min(half, 512)
        for n in range(half // step):
            pair = []
            for base in (0, half):
                part = None
                lo = base + n * step
                down = wd[:, :, lo : lo + step].reshape(local * hidden, step)
                part = jnp.dot(act[...], down, preferred_element_type=F32)
                pair.append(part.reshape(blocks, per, step))
            yb[pl.ds(first, blocks), :, n * step : (n + 1) * step] = jnp.concatenate(
                pair, axis=1
            ).astype(BF16)
        return carry

    lax.fori_loop(0, total // rows, experts, 0)

    def half_sum(kx):
        c = col_at(kx)
        src = pl.multiple_of((2 * c + 1 - core) * n_ex, n_ex)
        return remote(
            yb.at[pl.ds(src, n_ex)],
            cbuf.at[pl.ds(pl.multiple_of(c * n_ex, n_ex), n_ex)],
            c_send.at[kx],
            c_recv.at[kx],
            sibling,
        )

    def pair_sum(kx, kz):
        c, z = col_at(kx), z_at(kz)
        return yb[at(c, core, z)].astype(F32) + cbuf[c * n_ex + z].astype(F32)

    column_order = [*range(1, n_col), 0]
    for kx in column_order:
        half_sum(kx).start()
    for kx in range(1, n_col):
        half_sum(kx).wait_recv()
        sent.append(half_sum(kx))
        for kz in range(n_ex - 1, -1, -1):
            i = kx * n_ex + kz
            sxbuf[i] = pair_sum(kx, kz).astype(BF16)
            copy = remote(
                sxbuf.at[i], rxbuf.at[i], rx_send.at[i], rx_recv.at[i], at(col_at(kx), core, ex)
            )
            copy.start()
            sent.append(copy)
    half_sum(0).wait_recv()
    sent.append(half_sum(0))
    mine = None
    for kz in range(n_ex - 1, -1, -1):
        mine = pair_sum(0, kz)
        for kx in range(1, n_col):
            i = kx * n_ex + kz
            remote(
                sxbuf.at[i], rxbuf.at[i], rx_send.at[i], rx_recv.at[i], at(col_at(kx), core, ex)
            ).wait_recv()
            mine += rxbuf[i].astype(F32)
        if kz:
            szbuf[kz] = mine.astype(BF16)
            copy = remote(
                szbuf.at[kz], rzbuf.at[kz], rz_send.at[kz], rz_recv.at[kz], at(col, core, z_at(kz))
            )
            copy.start()
            sent.append(copy)
    for kz in range(1, n_ex):
        remote(
            szbuf.at[kz], rzbuf.at[kz], rz_send.at[kz], rz_recv.at[kz], at(col, core, z_at(kz))
        ).wait_recv()
        mine += rzbuf[kz].astype(F32)
    mixed_low = x[:, :half] + mine[:per]
    mixed_top = x[:, half:] + mine[per:]
    square = jnp.sum(mixed_low * mixed_low + mixed_top * mixed_top, axis=-1, keepdims=True)
    inverse = lax.rsqrt(square / width + epsilon)
    zbuf[me] = jnp.concatenate(
        [mixed_low * inverse * fg_ref[:, :half], mixed_top * inverse * fg_ref[:, half:]], axis=0
    ).astype(BF16)

    sent += gather(zbuf, z_z, z_x, z_c, z_recv)
    loads[3].wait()
    loads[4].wait()

    def head(r, carry):
        first = pl.multiple_of(r * blocks, blocks)
        span = pl.ds(pl.multiple_of(r * rows, rows), rows)
        packed = zbuf[pl.ds(first, blocks)].astype(F32)
        low = packed[:, 0:per, :].reshape(rows, half)
        top = packed[:, per : 2 * per, :].reshape(rows, half)
        inputs = jnp.concatenate([low, top], axis=1).astype(BF16)
        teacher = jnp.dot(inputs, hw[...], preferred_element_type=F32)
        teach[span, :] = teacher
        student = st[span, :].astype(F32)
        t_top = jnp.max(teacher, axis=1, keepdims=True)
        s_top = jnp.max(student, axis=1, keepdims=True)
        t_sum = jnp.sum(jnp.exp(teacher - t_top), axis=1, keepdims=True)
        s_exp = jnp.exp(student - s_top)
        s_sum = jnp.sum(s_exp, axis=1, keepdims=True)
        cross = jnp.sum(s_exp * (student - teacher), axis=1, keepdims=True)
        where = lax.broadcasted_iota(jnp.int32, (rows, LANES), 1)
        table = jnp.zeros((rows, LANES), F32)
        for i, value in enumerate((t_top, t_sum, s_top, s_sum, cross)):
            table = jnp.where(where == i, value, table)
        stat[me, :, span] = table.T[0:8]
        return carry

    lax.fori_loop(0, total // rows, head, 0)

    def tell(k):
        position = lax.rem(me + k, n_dev)
        return remote(stat.at[me], stat.at[me], s_send.at[k], s_recv.at[me], position)

    def heard(k):
        position = lax.rem(me + k, n_dev)
        return remote(stat.at[position], stat.at[position], s_send.at[0], s_recv.at[position], sibling)

    def tell_all(k, carry):
        tell(k).start()
        return carry

    def hear_all(k, carry):
        heard(k).wait_recv()
        return carry

    lax.fori_loop(1, n_dev, tell_all, 0)
    lax.fori_loop(1, n_dev, hear_all, 0)

    def final(r, carry):
        span = pl.ds(pl.multiple_of(r * rows, rows), rows)
        t_tops, t_sums = stat[:, 0, span], stat[:, 1, span]
        s_tops, s_sums, crosses = stat[:, 2, span], stat[:, 3, span], stat[:, 4, span]
        t_top = jnp.max(t_tops, axis=0, keepdims=True)
        s_top = jnp.max(s_tops, axis=0, keepdims=True)
        t_total = jnp.sum(jnp.exp(t_tops - t_top) * t_sums, axis=0, keepdims=True)
        s_scale = jnp.exp(s_tops - s_top)
        s_total = jnp.sum(s_scale * s_sums, axis=0, keepdims=True)
        cross = jnp.sum(s_scale * crosses, axis=0, keepdims=True)
        log_t = t_top + jnp.log(t_total)
        log_s = s_top + jnp.log(s_total)
        divergence = cross / s_total - log_s + log_t
        valid = valid_ref[:, span].astype(F32)
        kl_ref[:, span] = valid * divergence
        where = lax.broadcasted_iota(jnp.int32, (LANES, rows), 0)
        table = jnp.zeros((LANES, rows), F32)
        for i, value in enumerate((log_s, divergence - log_t + log_s, valid)):
            table = jnp.where(where == i, value, table)
        columns = table.T
        student = st[span, :].astype(F32)
        prob = columns[:, 2:3] * jnp.exp(student - columns[:, 0:1])
        grad_ref[span, :] = (prob * (student - teach[span, :] - columns[:, 1:2])).astype(BF16)
        return carry

    lax.fori_loop(0, total // rows, final, 0)

    for copy in sent:
        copy.wait_send()

    def finish_tell(k, carry):
        tell(k).wait_send()
        return carry

    lax.fori_loop(1, n_dev, finish_tell, 0)


def body(
    n_dp,
    n_ex,
    tokens,
    routes,
    gates,
    valid,
    norm_gain,
    final_gain,
    w_gate,
    w_up,
    w_down,
    head_weight,
    student_logits,
):
    per, width = tokens.shape
    half = width // 2
    n_dev = n_dp * n_ex
    n_chip = n_dev // 2
    n_col = n_dp // 2
    total, vocab = student_logits.shape
    local, _, hidden = w_gate.shape
    rows = min(total, 128)
    vmem = pl.BlockSpec(memory_space=pltpu.VMEM)
    hbm = pl.BlockSpec(memory_space=pl.ANY)
    dma = pltpu.SemaphoreType.DMA
    kl, grad = pl.pallas_call(
        functools.partial(kernel, n_dp, n_ex),
        out_shape=(
            jax.ShapeDtypeStruct((1, total), F32),
            jax.ShapeDtypeStruct((total, vocab), BF16),
        ),
        in_specs=[vmem] * 6 + [hbm] * 5,
        out_specs=(vmem, vmem),
        scratch_shapes=[
            pltpu.VMEM(w_gate.shape, BF16),
            pltpu.VMEM(w_up.shape, BF16),
            pltpu.VMEM(w_down.shape, BF16),
            pltpu.VMEM(head_weight.shape, BF16),
            pltpu.VMEM(student_logits.shape, BF16),
            pltpu.VMEM((n_dev, 2 * per, half + LANES), BF16),
            pltpu.VMEM((rows, local * hidden), BF16),
            pltpu.VMEM((n_dev, 2 * per, half), BF16),
            pltpu.VMEM((n_chip, 2 * per, half), BF16),
            pltpu.VMEM((n_chip, 2 * per, half), BF16),
            pltpu.VMEM((n_chip, 2 * per, half), BF16),
            pltpu.VMEM((n_ex, 2 * per, half), BF16),
            pltpu.VMEM((n_ex, 2 * per, half), BF16),
            pltpu.VMEM((n_dev, 2 * per, half), BF16),
            pltpu.VMEM((n_dev, 8, total), F32),
            pltpu.VMEM((total, vocab), F32),
            dma((5,)),
            dma((n_ex,)),
            dma((n_chip,)),
            dma((n_chip,)),
            dma((n_dev,)),
            dma((n_col,)),
            dma((n_col,)),
            dma((n_chip,)),
            dma((n_chip,)),
            dma((n_ex,)),
            dma((n_ex,)),
            dma((n_ex,)),
            dma((n_chip,)),
            dma((n_chip,)),
            dma((n_dev,)),
            dma((n_dev,)),
            dma((n_dev,)),
        ],
        compiler_params=pltpu.CompilerParams(
            collective_id=0, has_side_effects=True, vmem_limit_bytes=60 * 2**20
        ),
    )(
        tokens,
        routes.T,
        gates,
        valid.reshape(1, total),
        norm_gain.reshape(1, width),
        final_gain.reshape(1, width),
        w_gate,
        w_up,
        w_down,
        head_weight,
        student_logits,
    )
    return kl.reshape(total), grad


def solution(mesh):
    placed = (
        P(("groups", "dp", "expert"), None),
        P("groups", None),
        P(("groups", "dp", "expert"), None),
        P("groups"),
        P(),
        P(),
        P("expert", None, "dp"),
        P("expert", None, "dp"),
        P("expert", "dp", None),
        P(None, ("dp", "expert")),
        P("groups", ("dp", "expert")),
    )
    return jax.shard_map(
        functools.partial(body, mesh.shape["dp"], mesh.shape["expert"]),
        mesh=mesh,
        in_specs=placed,
        out_specs=(P("groups"), P("groups", ("dp", "expert"))),
        check_vma=False,
    )
```

```python
import functools

import jax
import jax.numpy as jnp
from jax import lax
from jax.experimental import pallas as pl
from jax.experimental.pallas import tpu as pltpu
from jax.sharding import PartitionSpec as P

epsilon = 1e-06
F32, BF16 = jnp.float32, jnp.bfloat16
LANES = 128


def kernel(
    n_dp,
    n_ex,
    tok_ref,
    routes_ref,
    gates_ref,
    valid_ref,
    ng_ref,
    fg_ref,
    wg_hbm,
    wu_hbm,
    wd_hbm,
    hw_hbm,
    st_hbm,
    teach,
    facts,
    wg,
    wu,
    wd,
    hw,
    st,
    xbuf,
    act,
    yb,
    cbuf,
    sxbuf,
    rxbuf,
    zbuf,
    stat,
    load_sem,
    x_z,
    x_x,
    x_c,
    x_recv,
    c_send,
    c_recv,
    rx_send,
    rx_recv,
    z_z,
    z_x,
    z_c,
    z_recv,
    s_send,
    s_recv,
):
    grp, dp, ex = lax.axis_index("groups"), lax.axis_index("dp"), lax.axis_index("expert")
    core = lax.rem(dp, 2)
    col = lax.div(dp, 2)
    n_dev = n_dp * n_ex
    n_col = n_dp // 2
    me = dp * n_ex + ex
    per, width = tok_ref.shape
    half = width // 2
    total = n_dev * per
    rows = min(total, 128)
    blocks = rows // per
    local = wg.shape[0]
    hidden = wg.shape[2]

    def device(position):
        return (grp, lax.div(position, n_ex), lax.rem(position, n_ex))

    def at(x_col, c, z):
        return (2 * x_col + c) * n_ex + z

    def col_at(k):
        return lax.rem(col + k, n_col)

    def z_at(k):
        out, bit = ex, 1
        while bit < n_ex:
            if k & bit:
                out = out + bit - 2 * bit * lax.rem(lax.div(ex, bit), 2)
            bit *= 2
        return out

    sibling = at(col, 1 - core, ex)

    def remote(src, dst, send, recv, position):
        return pltpu.make_async_remote_copy(
            src_ref=src,
            dst_ref=dst,
            send_sem=send,
            recv_sem=recv,
            device_id=device(position),
            device_id_type=pl.DeviceIdType.MESH,
        )

    loads = [
        pltpu.make_async_copy(src, dst, load_sem.at[i])
        for i, (src, dst) in enumerate(
            ((wg_hbm, wg), (wu_hbm, wu), (wd_hbm, wd), (st_hbm, st), (hw_hbm, hw))
        )
    ]
    for load in loads:
        load.start()

    barrier = pltpu.get_barrier_semaphore()

    def greet(k, carry):
        pl.semaphore_signal(
            barrier,
            inc=1,
            device_id=device(lax.rem(me + k, n_dev)),
            device_id_type=pl.DeviceIdType.MESH,
        )
        return carry

    lax.fori_loop(1, n_dev, greet, 0)

    x = tok_ref[...].astype(F32)
    normed = x * lax.rsqrt(jnp.mean(x * x, axis=-1, keepdims=True) + epsilon) * ng_ref[...]
    gates = gates_ref[...]
    weights = gates / jnp.sum(gates, axis=1, keepdims=True)
    lane = lax.broadcasted_iota(jnp.int32, (per, LANES), 1)
    spot = lax.broadcasted_iota(jnp.int32, (per, total), 1)
    own = spot == lax.broadcasted_iota(jnp.int32, (per, total), 0) + me * per
    dense = jnp.zeros((per, LANES), F32)
    for k in range(gates.shape[1]):
        route = jnp.sum(
            jnp.where(own, routes_ref[k : k + 1, :], 0).astype(F32), axis=1, keepdims=True
        )
        dense += jnp.where(lane.astype(F32) == route, weights[:, k : k + 1], 0.0)
    high = dense.astype(BF16).astype(F32)
    xbuf[me, :, 0:half] = jnp.concatenate([normed[:, :half], normed[:, half:]], axis=0).astype(BF16)
    xbuf[me, :, half : half + LANES] = jnp.concatenate([high, dense - high], axis=0).astype(BF16)

    pl.semaphore_wait(barrier, n_dev - 1)

    def gather(buf, send_z, send_x, send_c, recv):
        def move(position, sem, target):
            return remote(buf.at[position], buf.at[position], sem, recv.at[position], target)

        started = []

        def start(position, sem, target):
            copy = move(position, sem, target)
            copy.start()
            started.append(copy)

        def arrive(position):
            move(position, send_c.at[0], sibling).wait_recv()

        def to_columns(position, kz):
            for kx in range(1, n_col):
                start(position, send_x.at[kz * n_col + kx], at(col_at(kx), core, ex))

        def chips(order):
            for kz in order:
                for kx in range(n_col):
                    if kz or kx:
                        yield kz, kx

        for kz, kx in chips(range(n_ex - 1, -1, -1)):
            start(me, send_x.at[kz * n_col + kx], at(col_at(kx), core, z_at(kz)))
        start(me, send_c.at[0], sibling)
        for kz, kx in chips(range(n_ex)):
            position = at(col_at(n_col - kx), core, z_at(kz))
            arrive(position)
            start(position, send_c.at[kz * n_col + kx], sibling)
        for kz in range(n_ex):
            for kx in range(n_col):
                arrive(at(col_at(n_col - kx), 1 - core, z_at(kz)))
        return started

    sent = gather(xbuf, x_z, x_x, x_c, x_recv)

    loads[0].wait()
    loads[1].wait()
    loads[2].wait()

    def experts(r, carry):
        first = pl.multiple_of(r * blocks, blocks)
        packed = xbuf[pl.ds(first, blocks)].astype(F32)
        low = packed[:, 0:per, :].reshape(rows, half + LANES)
        top = packed[:, per : 2 * per, :].reshape(rows, half + LANES)
        inputs = jnp.concatenate([low[:, :half], top[:, :half]], axis=1).astype(BF16)
        scales = low[:, half:] + top[:, half:]
        where = lax.broadcasted_iota(jnp.int32, (rows, LANES), 1)
        for j in range(local):
            scale = jnp.sum(
                jnp.where(where == ex * local + j, scales, 0.0), axis=1, keepdims=True
            )
            gate = jnp.dot(inputs, wg[j], preferred_element_type=F32)
            up = jnp.dot(inputs, wu[j], preferred_element_type=F32)
            out = gate / (1.0 + jnp.exp(-gate)) * up * scale
            act[:, j * hidden : (j + 1) * hidden] = out.astype(BF16)
        step = min(half, 512)
        for n in range(half // step):
            pair = []
            for base in (0, half):
                part = None
                lo = base + n * step
                down = wd[:, :, lo : lo + step].reshape(local * hidden, step)
                part = jnp.dot(act[...], down, preferred_element_type=F32)
                pair.append(part.reshape(blocks, per, step))
            yb[pl.ds(first, blocks), :, n * step : (n + 1) * step] = jnp.concatenate(
                pair, axis=1
            ).astype(BF16)
        return carry

    lax.fori_loop(0, total // rows, experts, 0)

    def half_sum(kx):
        c = col_at(kx)
        src = pl.multiple_of((2 * c + 1 - core) * n_ex, n_ex)
        return remote(
            yb.at[pl.ds(src, n_ex)],
            cbuf.at[pl.ds(pl.multiple_of(c * n_ex, n_ex), n_ex)],
            c_send.at[kx],
            c_recv.at[kx],
            sibling,
        )

    def pair_sum(kx, kz):
        c, z = col_at(kx), z_at(kz)
        return yb[at(c, core, z)].astype(F32) + cbuf[c * n_ex + z].astype(F32)

    column_order = [*range(1, n_col), 0]
    for kx in column_order:
        half_sum(kx).start()
    for kx in column_order:
        half_sum(kx).wait_recv()
        sent.append(half_sum(kx))

    def scatter(kz, kx):
        i = kx * n_ex + kz
        return remote(
            sxbuf.at[i],
            rxbuf.at[i],
            rx_send.at[i],
            rx_recv.at[i],
            at(col_at(kx), core, z_at(kz)),
        )

    order = [(kz, kx) for kz in range(n_ex - 1, -1, -1) for kx in column_order if kz or kx]
    for kz, kx in order:
        sxbuf[kx * n_ex + kz] = pair_sum(kx, kz).astype(BF16)
        scatter(kz, kx).start()
        sent.append(scatter(kz, kx))
    mine = pair_sum(0, 0)
    for kz, kx in reversed(order):
        scatter(kz, kx).wait_recv()
        mine += rxbuf[kx * n_ex + kz].astype(F32)
    mixed_low = x[:, :half] + mine[:per]
    mixed_top = x[:, half:] + mine[per:]
    square = jnp.sum(mixed_low * mixed_low + mixed_top * mixed_top, axis=-1, keepdims=True)
    inverse = lax.rsqrt(square / width + epsilon)
    zbuf[me] = jnp.concatenate(
        [mixed_low * inverse * fg_ref[:, :half], mixed_top * inverse * fg_ref[:, half:]], axis=0
    ).astype(BF16)

    sent += gather(zbuf, z_z, z_x, z_c, z_recv)
    loads[3].wait()
    loads[4].wait()

    def head(r, carry):
        first = pl.multiple_of(r * blocks, blocks)
        span = pl.ds(pl.multiple_of(r * rows, rows), rows)
        packed = zbuf[pl.ds(first, blocks)].astype(F32)
        low = packed[:, 0:per, :].reshape(rows, half)
        top = packed[:, per : 2 * per, :].reshape(rows, half)
        inputs = jnp.concatenate([low, top], axis=1).astype(BF16)
        teacher = jnp.dot(inputs, hw[...], preferred_element_type=F32)
        teach[span, :] = teacher
        student = st[span, :].astype(F32)
        t_top = jnp.max(teacher, axis=1, keepdims=True)
        s_top = jnp.max(student, axis=1, keepdims=True)
        t_sum = jnp.sum(jnp.exp(teacher - t_top), axis=1, keepdims=True)
        s_exp = jnp.exp(student - s_top)
        s_sum = jnp.sum(s_exp, axis=1, keepdims=True)
        cross = jnp.sum(s_exp * (student - teacher), axis=1, keepdims=True)
        where = lax.broadcasted_iota(jnp.int32, (rows, LANES), 1)
        table = jnp.zeros((rows, LANES), F32)
        for i, value in enumerate((t_top, t_sum, s_top, s_sum, cross)):
            table = jnp.where(where == i, value, table)
        stat[me, :, span] = table.T[0:8]
        return carry

    lax.fori_loop(0, total // rows, head, 0)

    def tell(k):
        position = lax.rem(me + k, n_dev)
        return remote(stat.at[me], stat.at[me], s_send.at[k], s_recv.at[me], position)

    def heard(k):
        position = lax.rem(me + k, n_dev)
        return remote(stat.at[position], stat.at[position], s_send.at[0], s_recv.at[position], sibling)

    def tell_all(k, carry):
        tell(k).start()
        return carry

    def hear_all(k, carry):
        heard(k).wait_recv()
        return carry

    lax.fori_loop(1, n_dev, tell_all, 0)
    lax.fori_loop(1, n_dev, hear_all, 0)

    def final(r, carry):
        span = pl.ds(pl.multiple_of(r * rows, rows), rows)
        t_tops, t_sums = stat[:, 0, span], stat[:, 1, span]
        s_tops, s_sums, crosses = stat[:, 2, span], stat[:, 3, span], stat[:, 4, span]
        t_top = jnp.max(t_tops, axis=0, keepdims=True)
        s_top = jnp.max(s_tops, axis=0, keepdims=True)
        t_total = jnp.sum(jnp.exp(t_tops - t_top) * t_sums, axis=0, keepdims=True)
        s_scale = jnp.exp(s_tops - s_top)
        s_total = jnp.sum(s_scale * s_sums, axis=0, keepdims=True)
        cross = jnp.sum(s_scale * crosses, axis=0, keepdims=True)
        log_t = t_top + jnp.log(t_total)
        log_s = s_top + jnp.log(s_total)
        divergence = cross / s_total - log_s + log_t
        valid = valid_ref[:, span].astype(F32)
        for i, value in enumerate((log_s, divergence - log_t + log_s, valid, valid * divergence)):
            facts[i : i + 1, span] = value
        return carry

    lax.fori_loop(0, total // rows, final, 0)

    for copy in sent:
        copy.wait_send()

    def finish_tell(k, carry):
        tell(k).wait_send()
        return carry

    lax.fori_loop(1, n_dev, finish_tell, 0)


def finish(teach, st, facts, kl_ref, grad_ref):
    total = teach.shape[0]
    rows = min(total, 128)
    kl_ref[...] = facts[3:4, :]

    def part(r, carry):
        span = pl.ds(pl.multiple_of(r * rows, rows), rows)
        where = lax.broadcasted_iota(jnp.int32, (LANES, rows), 0)
        table = jnp.zeros((LANES, rows), F32)
        for i in range(3):
            table = jnp.where(where == i, facts[i : i + 1, span], table)
        columns = table.T
        student = st[span, :].astype(F32)
        prob = columns[:, 2:3] * jnp.exp(student - columns[:, 0:1])
        grad_ref[span, :] = (prob * (student - teach[span, :] - columns[:, 1:2])).astype(BF16)
        return carry

    lax.fori_loop(0, total // rows, part, 0)


def body(
    n_dp,
    n_ex,
    tokens,
    routes,
    gates,
    valid,
    norm_gain,
    final_gain,
    w_gate,
    w_up,
    w_down,
    head_weight,
    student_logits,
):
    per, width = tokens.shape
    half = width // 2
    n_dev = n_dp * n_ex
    n_chip = n_dev // 2
    n_col = n_dp // 2
    total, vocab = student_logits.shape
    local, _, hidden = w_gate.shape
    rows = min(total, 128)
    vmem = pl.BlockSpec(memory_space=pltpu.VMEM)
    hbm = pl.BlockSpec(memory_space=pl.ANY)
    dma = pltpu.SemaphoreType.DMA
    teacher, facts = pl.pallas_call(
        functools.partial(kernel, n_dp, n_ex),
        out_shape=(
            jax.ShapeDtypeStruct((total, vocab), F32),
            jax.ShapeDtypeStruct((4, total), F32),
        ),
        in_specs=[vmem] * 6 + [hbm] * 5,
        out_specs=(vmem, vmem),
        scratch_shapes=[
            pltpu.VMEM(w_gate.shape, BF16),
            pltpu.VMEM(w_up.shape, BF16),
            pltpu.VMEM(w_down.shape, BF16),
            pltpu.VMEM(head_weight.shape, BF16),
            pltpu.VMEM(student_logits.shape, BF16),
            pltpu.VMEM((n_dev, 2 * per, half + LANES), BF16),
            pltpu.VMEM((rows, local * hidden), BF16),
            pltpu.VMEM((n_dev, 2 * per, half), BF16),
            pltpu.VMEM((n_chip, 2 * per, half), BF16),
            pltpu.VMEM((n_chip, 2 * per, half), BF16),
            pltpu.VMEM((n_chip, 2 * per, half), BF16),
            pltpu.VMEM((n_dev, 2 * per, half), BF16),
            pltpu.VMEM((n_dev, 8, total), F32),
            dma((5,)),
            dma((n_ex,)),
            dma((n_chip,)),
            dma((n_chip,)),
            dma((n_dev,)),
            dma((n_col,)),
            dma((n_col,)),
            dma((n_chip,)),
            dma((n_chip,)),
            dma((n_ex,)),
            dma((n_chip,)),
            dma((n_chip,)),
            dma((n_dev,)),
            dma((n_dev,)),
            dma((n_dev,)),
        ],
        compiler_params=pltpu.CompilerParams(
            collective_id=0, has_side_effects=True, vmem_limit_bytes=60 * 2**20
        ),
    )(
        tokens,
        routes.T,
        gates,
        valid.reshape(1, total),
        norm_gain.reshape(1, width),
        final_gain.reshape(1, width),
        w_gate,
        w_up,
        w_down,
        head_weight,
        student_logits,
    )
    kl, grad = pl.pallas_call(
        finish,
        out_shape=(
            jax.ShapeDtypeStruct((1, total), F32),
            jax.ShapeDtypeStruct((total, vocab), BF16),
        ),
        in_specs=[vmem] * 3,
        out_specs=(vmem, vmem),
        compiler_params=pltpu.CompilerParams(vmem_limit_bytes=24 * 2**20),
    )(teacher, student_logits, facts)
    return kl.reshape(total), grad


def solution(mesh):
    placed = (
        P(("groups", "dp", "expert"), None),
        P("groups", None),
        P(("groups", "dp", "expert"), None),
        P("groups"),
        P(),
        P(),
        P("expert", None, "dp"),
        P("expert", None, "dp"),
        P("expert", "dp", None),
        P(None, ("dp", "expert")),
        P("groups", ("dp", "expert")),
    )
    return jax.shard_map(
        functools.partial(body, mesh.shape["dp"], mesh.shape["expert"]),
        mesh=mesh,
        in_specs=placed,
        out_specs=(P("groups"), P("groups", ("dp", "expert"))),
        check_vma=False,
    )
```
